256 devices in a mesh: pipe: 8 (over x, core), tensor: 32 (over y, z).
Axes of the slice: x: 4, y: 4, z: 8, core: 2. Of those that a mesh axis runs over, the one named last changes fastest.
Arguments:
- x_in: bfloat16 [4, 64, 7168], P(None, None, 'tensor'), may hold values from -6 to 6
- cotangent: bfloat16 [4, 64, 7168], P(None, None, 'tensor'), may hold values from -6 to 6
- w_in: bfloat16 [8, 6, 224, 28672], P('pipe', None, None, 'tensor'), may hold values from -0.15625 to 0.15625
- w_out: bfloat16 [8, 6, 896, 7168], P('pipe', None, None, 'tensor'), may hold values from -0.078125 to 0.078125
Outputs:
- grad_acts: bfloat16 [8, 4, 64, 7168], P('pipe', None, None, 'tensor')
- grad_w_in: bfloat16 [8, 6, 224, 28672], P('pipe', None, None, 'tensor')
- grad_w_out: bfloat16 [8, 6, 896, 7168], P('pipe', None, None, 'tensor')
The draws below stay inside these ranges and needn't reach their ends.
All inputs are finite; a program needn't handle non-finite values.
Results may differ from the reference program's by a relative error of at most 0.04.
Values may be sent and summed in bfloat16 or wider, within the bound.
No kernel may reach another device: no remote copies, remote signals or barrier semaphores. Data moves between devices by JAX's collectives and lax.ppermute only.
A program may use at most 64 MiB of HBM per device.

```python
import jax
import jax.numpy as jnp
from jax import lax

D = 7168
FF = 28672
TOK = 64
MB = 4
LEVELS = 5
D_SLAB = 224
H_SLAB = 896
N_PIPE = 8
N_TENSOR = 32


def levels(own_key, dims, split, smallest, high):
    def one(axis_at, parts):
        steps = jax.random.uniform(jax.random.fold_in(jax.random.fold_in(own_key, 6), axis_at), (parts,), jnp.float32, smallest / len(split), high / len(split))
        return jnp.repeat(jnp.exp(steps), dims[axis_at] // parts).reshape((-1,) + (1,) * (len(dims) - axis_at - 1))

    level = one(*split[0])
    for cut in split[1:]:
        level = level * one(*cut)
    return level


def bell_draw(key, shape, spread, bound, shards=(), kind=jnp.bfloat16):
    values = spread * jax.random.normal(key, shape, jnp.float32)
    if shards:
        values = values * levels(key, shape, shards, -0.22, 0.18)
    return jnp.clip(values, -bound, bound).astype(kind)


def setup_inputs(seed: int = 0) -> dict:
    splits = jax.random.split(jax.random.key(seed), 5)
    x_in = bell_draw(splits[0], (MB, TOK, D), 1.0, 6.0, ((2, 32),))
    cotangent = bell_draw(splits[1], (MB, TOK, D), 1.0, 6.0, ((2, 32),))
    w_in = bell_draw(splits[2], (N_PIPE, LEVELS + 1, D_SLAB, FF), ((LEVELS + 1) * D_SLAB) ** -0.5, 0.15625, ((0, 8), (3, 32)))
    w_out = bell_draw(splits[3], (N_PIPE, LEVELS + 1, H_SLAB, D), ((LEVELS + 1) * H_SLAB) ** -0.5, 0.078125, ((0, 8), (3, 32)))
    return dict(x_in=x_in, cotangent=cotangent, w_in=w_in, w_out=w_out)


def gelu_value(values):
    return jax.nn.gelu(values, approximate=True)

def gelu_slope(preact):
    result, pullback = jax.vjp(gelu_value, preact)
    return pullback(jnp.ones_like(preact))[0]

def rounded(values):
    return lax.optimization_barrier(values.astype(jnp.bfloat16)).astype(jnp.float32)

def to_slabs(array, slab_width):
    return array.astype(jnp.float32).reshape(MB, TOK, N_TENSOR, slab_width).transpose(0, 2, 1, 3)

def from_slabs(array):
    return array.transpose(0, 2, 1, 3).reshape(MB, TOK, N_TENSOR * array.shape[3])

def reference(x_in, cotangent, w_in, w_out):
    n_terms = LEVELS + 1
    slab_ids = jnp.arange(N_TENSOR, dtype=jnp.int32)
    partner = [slab_ids] + [jnp.bitwise_xor(slab_ids, jnp.int32(1 << level)) for level in range(LEVELS)]

    def blocks(layer_no):
        w_first = w_in[layer_no].astype(jnp.float32).reshape(n_terms, D_SLAB, N_TENSOR, H_SLAB).transpose(0, 2, 1, 3)
        w_second = w_out[layer_no].astype(jnp.float32).reshape(n_terms, H_SLAB, N_TENSOR, D_SLAB).transpose(0, 2, 1, 3)
        return (w_first, w_second)
    activity = to_slabs(x_in, D_SLAB)
    stored = []
    for layer_no in range(N_PIPE):
        w_first, w_second = blocks(layer_no)
        preact = sum((jnp.einsum('mntd,ndf->mntf', activity[:, partner[term]], w_first[term]) for term in range(n_terms)))
        hidden = rounded(gelu_value(preact))
        layer_out = activity + sum((jnp.einsum('mntf,nfd->mntd', hidden[:, partner[term]], w_second[term]) for term in range(n_terms)))
        stored.append((activity, preact, hidden))
        activity = rounded(layer_out)
    gradient = to_slabs(cotangent, D_SLAB)
    grad_list = [None] * N_PIPE
    first_list = [None] * N_PIPE
    second_list = [None] * N_PIPE
    for layer_no in reversed(range(N_PIPE)):
        activity, preact, hidden = stored[layer_no]
        w_first, w_second = blocks(layer_no)
        hid_grad = sum((rounded(jnp.einsum('mntd,nfd->mntf', gradient, w_second[term]))[:, partner[term]] for term in range(n_terms)))
        dpre = rounded(hid_grad * gelu_slope(preact))
        input_grad = gradient + sum((rounded(jnp.einsum('mntf,ndf->mntd', dpre, w_first[term]))[:, partner[term]] for term in range(n_terms)))
        first_terms = []
        second_terms = []
        for term in range(n_terms):
            g_first = jnp.einsum('mntd,mntf->ndf', activity[:, partner[term]], dpre)
            first_terms.append(g_first.transpose(1, 0, 2).reshape(D_SLAB, FF))
            g_second = jnp.einsum('mntf,mntd->nfd', hidden[:, partner[term]], gradient)
            second_terms.append(g_second.transpose(1, 0, 2).reshape(H_SLAB, D))
        first_list[layer_no] = jnp.stack(first_terms).astype(jnp.bfloat16)
        second_list[layer_no] = jnp.stack(second_terms).astype(jnp.bfloat16)
        grad_list[layer_no] = from_slabs(input_grad).astype(jnp.bfloat16)
        gradient = rounded(input_grad)
    return (jnp.stack(grad_list), jnp.stack(first_list), jnp.stack(second_list))
```

```python
import functools

import jax
import jax.numpy as jnp
from jax import lax
from jax.experimental import pallas as pl
from jax.experimental.pallas import tpu as pltpu
from jax.sharding import PartitionSpec as P

AXES = ("pipe", "tensor")
GELU_C = 0.7978845608028654
GELU_A = 0.044715
VMEM = pl.BlockSpec(memory_space=pltpu.VMEM)
SMEM = pl.BlockSpec(memory_space=pltpu.SMEM)
F32 = jnp.float32
BF16 = jnp.bfloat16


def partner(index, term):
    return index if term == 0 else index ^ (1 << (term - 1))


def send(value, term, routes):
    width = lax.axis_size("tensor")
    pairs = [
        (a * width + i, b * width + partner(i, term)) for a, b in routes for i in range(width)
    ]
    return lax.ppermute(value, AXES, pairs)


def column_chunks(width):
    return [(start, min(256, width - start)) for start in range(0, width, 256)]


def dot_nn(a, b):
    return lax.dot_general(a, b, (((1,), (0,)), ((), ())), preferred_element_type=F32)


def dot_nt(a, b):
    return lax.dot_general(a, b, (((1,), (1,)), ((), ())), preferred_element_type=F32)


def dot_tn(a, b):
    return lax.dot_general(a, b, (((0,), (0,)), ((), ())), preferred_element_type=F32)


def forward_kernel(n, last, *refs):
    active = refs[0]
    ins = refs[1 : 1 + n]
    first = refs[1 + n]
    second = refs[2 + n : 2 + 2 * n]
    preact, hidden = refs[2 + 2 * n : 4 + 2 * n]
    outs = refs[4 + 2 * n :]

    @pl.when(active[0] == 1)
    def _():
        for start, size in column_chunks(preact.shape[1]):
            cols = slice(start, start + size)
            total = dot_nn(ins[0][...], first[0, :, cols])
            for k in range(1, n):
                total = total + dot_nn(ins[k][...], first[k, :, cols])
            preact[:, cols] = total
            inner = GELU_C * (total + GELU_A * (total * total * total))
            hidden[:, cols] = (0.5 * total * (1.0 + jnp.tanh(inner))).astype(BF16)
        if not last:
            outs[0][...] = ins[0][...].astype(F32) + dot_nt(hidden[...], second[0][...])
            for k in range(1, n):
                outs[k][...] = dot_nt(hidden[...], second[k][...]).astype(BF16)


def backward_kernel(n, *refs):
    active = refs[0]
    ins = refs[1 : 1 + n]
    first = refs[1 + n]
    second = refs[2 + n : 2 + 2 * n]
    preact = refs[2 + 2 * n]
    dpre = refs[3 + 2 * n]
    outs = refs[4 + 2 * n :]

    @pl.when(active[0] == 1)
    def _():
        for start, size in column_chunks(preact.shape[1]):
            cols = slice(start, start + size)
            total = dot_nn(ins[0][...], second[0][:, cols])
            for k in range(1, n):
                total = total + dot_nn(ins[k][...], second[k][:, cols])
            x = preact[:, cols]
            square = x * x
            bent = jnp.tanh(GELU_C * (x + GELU_A * (square * x)))
            slope = 0.5 * (1.0 + bent) + 0.5 * x * (1.0 - bent * bent) * (
                GELU_C * (1.0 + 3.0 * GELU_A * square)
            )
            dpre[:, cols] = (total * slope).astype(BF16)
        outs[0][...] = ins[0][...].astype(F32) + dot_nt(dpre[...], first[0])
        for k in range(1, n):
            outs[k][...] = dot_nt(dpre[...], first[k]).astype(BF16)


def grad_kernel(n, *refs):
    ins = refs[:n]
    dpre = refs[n]
    hiddens = refs[n + 1 : 2 * n + 1]
    grad = refs[2 * n + 1]
    out_first, out_second = refs[2 * n + 2 :]
    for k in range(n):
        out_first[k] = dot_tn(ins[k][...], dpre[...]).astype(BF16)
        out_second[k] = dot_tn(grad[...], hiddens[k][...]).astype(BF16)


def call(kernel, out_shapes, args, flops, touched, flagged=True):
    return pl.pallas_call(
        kernel,
        out_shape=out_shapes,
        in_specs=([SMEM] if flagged else []) + [VMEM] * (len(args) - flagged),
        out_specs=[VMEM] * len(out_shapes),
        cost_estimate=pl.CostEstimate(flops=flops, bytes_accessed=touched, transcendentals=0),
        compiler_params=pltpu.CompilerParams(vmem_limit_bytes=24 * 1024 * 1024),
    )(*args)


def body(x_in, cotangent, w_in, w_out):
    sections = lax.axis_size("pipe")
    n = lax.axis_size("tensor").bit_length()
    me = lax.axis_index("pipe")
    batches, tok_rows, slab = x_in.shape
    tokens = batches * tok_rows
    first = w_in[0]
    owned = jnp.swapaxes(w_out[0], 1, 2)
    hid = first.shape[2]
    shape = jax.ShapeDtypeStruct
    flops = 4 * tokens * n * slab * hid
    touched = 4 * n * slab * hid

    x = x_in.reshape(tokens, slab)
    cot = cotangent.reshape(tokens, slab)
    everyone = [(s, s) for s in range(sections)]
    order = [k for k in (3, 5, 2, 4, 1) if k < n]

    def exchange(values, routes):
        got = {k: send(values[k], k, routes) for k in order}
        return [got[k] for k in range(1, n)]

    ins = [x] + exchange([x] * n, everyone)
    second_0 = [owned[0]] + exchange(owned, [(0, 0)])
    second_r = [owned[0]] + exchange(owned, everyone[1:])
    grads_in = [cot] + exchange([cot] * n, everyone)

    saved_ins = list(ins)
    saved_pre = saved_hid = None
    for layer in range(sections):
        last = layer == sections - 1
        active = (me == layer).astype(jnp.int32).reshape(1)
        second = second_0 if layer == 0 else second_r
        shapes = [shape((tokens, hid), F32), shape((tokens, hid), BF16)]
        if not last:
            shapes += [shape((tokens, slab), F32)] + [shape((tokens, slab), BF16)] * (n - 1)
        preact, hidden, *terms = call(
            functools.partial(forward_kernel, n, last),
            shapes,
            [active] + ins + [first] + second,
            flops // (2 if last else 1),
            touched,
        )
        if layer == 0:
            saved_pre, saved_hid = preact, hidden
        else:
            mine = me == layer
            saved_ins = [jnp.where(mine, a, b) for a, b in zip(ins, saved_ins)]
            saved_pre = jnp.where(mine, preact, saved_pre)
            saved_hid = jnp.where(mine, hidden, saved_hid)
        if last:
            break
        total = terms[0]
        for got in exchange(terms, everyone):
            total = total + got.astype(F32)
        out = total.astype(BF16)
        route = [(layer, layer + 1)]
        ins = exchange([out] * n, route)
        ins = [send(out, 0, route)] + ins

    hiddens = [saved_hid] + exchange([saved_hid] * n, everyone)

    saved_grad = cot
    saved_dpre = saved_out = None
    for layer in reversed(range(sections)):
        active = (me == layer).astype(jnp.int32).reshape(1)
        second = second_0 if layer == 0 else second_r
        dpre, *terms = call(
            functools.partial(backward_kernel, n),
            [shape((tokens, hid), BF16), shape((tokens, slab), F32)]
            + [shape((tokens, slab), BF16)] * (n - 1),
            [active] + grads_in + [first] + second + [saved_pre],
            flops,
            touched,
        )
        total = terms[0]
        for got in exchange(terms, everyone):
            total = total + got.astype(F32)
        out = total.astype(BF16)
        if layer == sections - 1:
            saved_dpre, saved_out = dpre, out
        else:
            mine = me == layer
            saved_grad = jnp.where(mine, grads_in[0], saved_grad)
            saved_dpre = jnp.where(mine, dpre, saved_dpre)
            saved_out = jnp.where(mine, out, saved_out)
        if layer > 0:
            route = [(layer, layer - 1)]
            grads_in = exchange([out] * n, route)
            grads_in = [send(out, 0, route)] + grads_in

    grad_first, grad_second = call(
        functools.partial(grad_kernel, n),
        [shape((n, slab, hid), BF16)] * 2,
        saved_ins + [saved_dpre] + hiddens + [saved_grad],
        flops,
        touched,
        flagged=False,
    )
    acts = saved_out.reshape(batches, tok_rows, slab)
    return acts[None], grad_first[None], jnp.swapaxes(grad_second, 1, 2)[None]


def solution(mesh):
    placed = (
        P(None, None, "tensor"),
        P(None, None, "tensor"),
        P("pipe", None, None, "tensor"),
        P("pipe", None, None, "tensor"),
    )
    return jax.shard_map(
        body,
        mesh=mesh,
        in_specs=placed,
        out_specs=(P("pipe", None, None, "tensor"),) * 3,
        check_vma=False,
    )
```

```python
import functools

import jax
import jax.numpy as jnp
from jax import lax
from jax.experimental import pallas as pl
from jax.experimental.pallas import tpu as pltpu
from jax.sharding import PartitionSpec as P

AXES = ("pipe", "tensor")
GELU_C = 0.7978845608028654
GELU_A = 0.044715
VMEM = pl.BlockSpec(memory_space=pltpu.VMEM)
SMEM = pl.BlockSpec(memory_space=pltpu.SMEM)
ANY = pl.BlockSpec(memory_space=pl.ANY)
F32 = jnp.float32
BF16 = jnp.bfloat16


def partner(index, term):
    return index if term == 0 else index ^ (1 << (term - 1))


def send(value, term, routes):
    width = lax.axis_size("tensor")
    pairs = [
        (a * width + i, b * width + partner(i, term)) for a, b in routes for i in range(width)
    ]
    return lax.ppermute(value, AXES, pairs)


def column_chunks(width):
    return [(start, min(256, width - start)) for start in range(0, width, 256)]


def dot_nn(a, b):
    return lax.dot_general(a, b, (((1,), (0,)), ((), ())), preferred_element_type=F32)


def dot_nt(a, b):
    return lax.dot_general(a, b, (((1,), (1,)), ((), ())), preferred_element_type=F32)


def dot_tn(a, b):
    return lax.dot_general(a, b, (((0,), (0,)), ((), ())), preferred_element_type=F32)


def copy_in(n, first, second, w_first, w_second, sems):
    copies = []
    for k in range(n):
        copies.append(pltpu.make_async_copy(first.at[k], w_first.at[k], sems.at[k]))
        copies.append(pltpu.make_async_copy(second[k], w_second.at[k], sems.at[n + k]))
    return copies[0::2], copies[1::2]


def forward_kernel(n, last, tokens, n_state, *refs):
    active, refs = refs[0], refs[1:]
    ins, refs = refs[:n], refs[n:]
    first, refs = refs[0], refs[1:]
    second, refs = refs[:n], refs[n:]
    refs = refs[n_state:]
    st_ins, st_pre, st_hid = refs[:3]
    outs, refs = (refs[3:3], refs[3:]) if last else (refs[3 : 3 + n], refs[3 + n :])
    w_first, w_second, preact, hidden, sems = refs
    rows = pl.ds(0, tokens)

    @pl.when(active[0] == 1)
    def _():
        from_first, from_second = copy_in(n, first, second, w_first, w_second, sems)
        for copy in from_first:
            copy.start()
        if not last:
            for copy in from_second:
                copy.start()
        saves = [
            pltpu.make_async_copy(ins[k].at[rows], st_ins.at[k], sems.at[2 * n + k])
            for k in range(n)
        ]
        for copy in saves:
            copy.start()
        for start, size in column_chunks(preact.shape[1]):
            cols = slice(start, start + size)
            total = None
            for k in range(n):
                if start == 0:
                    from_first[k].wait()
                part = dot_nn(ins[k][rows, :], w_first[k, :, cols])
                total = part if k == 0 else total + part
            preact[:, cols] = total
            inner = GELU_C * (total + GELU_A * (total * total * total))
            hidden[:, cols] = (0.5 * total * (1.0 + jnp.tanh(inner))).astype(BF16)
        saves.append(pltpu.make_async_copy(preact, st_pre, sems.at[3 * n]))
        saves.append(pltpu.make_async_copy(hidden, st_hid, sems.at[3 * n + 1]))
        saves[n].start()
        saves[n + 1].start()
        if not last:
            for k in range(n):
                from_second[k].wait()
                part = dot_nt(hidden[...], w_second[k])
                if k == 0:
                    outs[0][...] = ins[0][rows, :].astype(F32) + part
                else:
                    outs[k][...] = part.astype(BF16)
        for copy in saves:
            copy.wait()


def backward_kernel(n, tokens, offset, n_state, *refs):
    active, refs = refs[0], refs[1:]
    ins, refs = refs[:n], refs[n:]
    first, refs = refs[0], refs[1:]
    second, refs = refs[:n], refs[n:]
    st_pre, refs = refs[0], refs[1 + n_state :]
    st_dpre, st_grad = refs[:2]
    outs, refs = refs[2 : 2 + n], refs[2 + n :]
    w_first, w_second, preact, dpre, sems = refs
    rows = pl.ds(offset, tokens)

    @pl.when(active[0] == 1)
    def _():
        from_first, from_second = copy_in(n, first, second, w_first, w_second, sems)
        from_pre = pltpu.make_async_copy(st_pre, preact, sems.at[2 * n])
        for copy in from_second + [from_pre] + from_first:
            copy.start()
        save_grad = pltpu.make_async_copy(ins[0].at[rows], st_grad, sems.at[2 * n + 1])
        save_grad.start()
        for start, size in column_chunks(preact.shape[1]):
            cols = slice(start, start + size)
            total = None
            for k in range(n):
                if start == 0:
                    from_second[k].wait()
                part = dot_nn(ins[k][rows, :], w_second[k, :, cols])
                total = part if k == 0 else total + part
            if start == 0:
                from_pre.wait()
            x = preact[:, cols]
            square = x * x
            bent = jnp.tanh(GELU_C * (x + GELU_A * (square * x)))
            slope = 0.5 * (1.0 + bent) + 0.5 * x * (1.0 - bent * bent) * (
                GELU_C * (1.0 + 3.0 * GELU_A * square)
            )
            dpre[:, cols] = (total * slope).astype(BF16)
        save_dpre = pltpu.make_async_copy(dpre, st_dpre, sems.at[2 * n + 2])
        save_dpre.start()
        for k in range(n):
            from_first[k].wait()
            part = dot_nt(dpre[...], w_first[k])
            if k == 0:
                outs[0][...] = ins[0][rows, :].astype(F32) + part
            else:
                outs[k][...] = part.astype(BF16)
        save_grad.wait()
        save_dpre.wait()


def grad_kernel(n, *refs):
    ins, dpre, refs = refs[0], refs[1], refs[2:]
    hiddens, grad, refs = refs[:n], refs[n], refs[n + 1 :]
    out_first, out_second, v_first, v_second, sems = refs
    copies = []
    for k in range(n):
        v_first[k] = dot_tn(ins[k], dpre[...]).astype(BF16)
        v_second[k] = dot_tn(grad[...], hiddens[k][...]).astype(BF16)
        copies.append(pltpu.make_async_copy(v_first.at[k], out_first.at[k], sems.at[k]))
        copies.append(pltpu.make_async_copy(v_second.at[k], out_second.at[k], sems.at[n + k]))
        copies[-2].start()
        copies[-1].start()
    for copy in copies:
        copy.wait()


def body(x_in, cotangent, w_in, w_out):
    sections = lax.axis_size("pipe")
    n = lax.axis_size("tensor").bit_length()
    me = lax.axis_index("pipe")
    batches, tok_rows, slab = x_in.shape
    tokens = batches * tok_rows
    first = w_in[0]
    owned = jnp.swapaxes(w_out[0], 1, 2)
    hid = first.shape[2]
    shape = jax.ShapeDtypeStruct
    cost = pl.CostEstimate(
        flops=4 * tokens * n * slab * hid, bytes_accessed=4 * n * slab * hid, transcendentals=0
    )
    params = pltpu.CompilerParams(vmem_limit_bytes=52 * 1024 * 1024)
    weights = [pltpu.VMEM((n, slab, hid), BF16)] * 2
    work = [pltpu.VMEM((tokens, hid), F32), pltpu.VMEM((tokens, hid), BF16)]
    term_shapes = [shape((tokens, slab), F32)] + [shape((tokens, slab), BF16)] * (n - 1)

    everyone = [(s, s) for s in range(sections)]
    order = [k for k in (3, 5, 2, 4, 1) if k < n]

    def exchange(values, routes):
        got = {k: send(values[k], k, routes) for k in order}
        return [got[k] for k in range(1, n)]

    def neighbours(layer, step):
        return [
            (s, s + step)
            for s in range(layer % 2, sections, 2)
            if 0 <= s + step < sections
        ]

    def reduced(terms, got):
        total = terms[0]
        for k in order:
            total = total + got[k - 1].astype(F32)
        return total.astype(BF16)

    both = jnp.concatenate(
        [x_in.reshape(tokens, slab), cotangent.reshape(tokens, slab)], axis=0
    )
    ins = [both] + exchange([both] * n, everyone)
    first_grads = ins
    second_0 = [owned[0]] + exchange(owned, [(0, 0)])
    second_r = None

    state = []
    for layer in range(sections):
        last = layer == sections - 1
        active = (me == layer).astype(jnp.int32).reshape(1)
        second = second_0 if layer == 0 else second_r
        state_shapes = [
            shape((n, tokens, slab), BF16), shape((tokens, hid), F32), shape((tokens, hid), BF16)
        ]
        outs = [] if last else term_shapes
        *state, = pl.pallas_call(
            functools.partial(forward_kernel, n, last, tokens, len(state)),
            out_shape=state_shapes + outs,
            in_specs=[SMEM] + [VMEM] * n + [ANY] * (1 + n + len(state)),
            out_specs=[ANY] * 3 + [VMEM] * len(outs),
            scratch_shapes=weights + work + [pltpu.SemaphoreType.DMA((3 * n + 2,))],
            input_output_aliases={2 + 2 * n + i: i for i in range(len(state))},
            cost_estimate=cost,
            compiler_params=params,
        )(active, *ins, first, *second, *state)
        state, terms = state[:3], state[3:]
        if last:
            break
        out = reduced(terms, exchange(terms, everyone))
        if layer == 0:
            second_r = [owned[0]] + exchange(owned, everyone)
        route = neighbours(layer, 1)
        ins = exchange([out] * n, route)
        ins = [send(out, 0, route)] + ins

    st_ins, st_pre, st_hid = state
    hiddens = {0: st_hid}
    pending = list(order)
    state = []
    grads_in = first_grads
    saved_out = None
    for layer in reversed(range(sections)):
        active = (me == layer).astype(jnp.int32).reshape(1)
        second = second_0 if layer == 0 else second_r
        st_dpre, st_grad, *terms = pl.pallas_call(
            functools.partial(
                backward_kernel, n, tokens, tokens if layer == sections - 1 else 0, len(state)
            ),
            out_shape=[shape((tokens, hid), BF16), shape((tokens, slab), BF16)] + term_shapes,
            in_specs=[SMEM] + [VMEM] * n + [ANY] * (2 + n + len(state)),
            out_specs=[ANY] * 2 + [VMEM] * n,
            scratch_shapes=weights + work + [pltpu.SemaphoreType.DMA((2 * n + 3,))],
            input_output_aliases={3 + 2 * n + i: i for i in range(len(state))},
            cost_estimate=cost,
            compiler_params=params,
        )(active, *grads_in, first, *second, st_pre, *state)
        state = [st_dpre, st_grad]
        out = reduced(terms, exchange(terms, everyone))
        saved_out = out if saved_out is None else jnp.where(me == layer, out, saved_out)
        if layer > 0:
            route = neighbours(layer, -1)
            grads_in = exchange([out] * n, route)
            grads_in = [send(out, 0, route)] + grads_in
            if pending and layer <= sections - 2:
                k = pending.pop(0)
                block, _ = lax.optimization_barrier((st_hid, out))
                hiddens[k] = send(block, k, everyone)
            if layer <= sections - 4:
                done = [k for k in hiddens if k]
                tied = lax.optimization_barrier(tuple(grads_in) + tuple(hiddens[k] for k in done))
                grads_in = list(tied[:n])
                hiddens.update(zip(done, tied[n:]))

    grad_first, grad_second = pl.pallas_call(
        functools.partial(grad_kernel, n),
        out_shape=[shape((n, slab, hid), BF16)] * 2,
        in_specs=[VMEM] * (3 + n),
        out_specs=[ANY] * 2,
        scratch_shapes=weights + [pltpu.SemaphoreType.DMA((2 * n,))],
        cost_estimate=cost,
        compiler_params=params,
    )(st_ins, st_dpre, *[hiddens[k] for k in range(n)], st_grad)
    acts = saved_out.reshape(batches, tok_rows, slab)
    return acts[None], grad_first[None], jnp.swapaxes(grad_second, 1, 2)[None]


def solution(mesh):
    placed = (
        P(None, None, "tensor"),
        P(None, None, "tensor"),
        P("pipe", None, None, "tensor"),
        P("pipe", None, None, "tensor"),
    )
    return jax.shard_map(
        body,
        mesh=mesh,
        in_specs=placed,
        out_specs=(P("pipe", None, None, "tensor"),) * 3,
        check_vma=False,
    )
```

```python
import functools

import jax
import jax.numpy as jnp
from jax import lax
from jax.experimental import pallas as pl
from jax.experimental.pallas import tpu as pltpu
from jax.sharding import PartitionSpec as P

AXES = ("pipe", "tensor")
GELU_C = 0.7978845608028654
GELU_A = 0.044715
VMEM = pl.BlockSpec(memory_space=pltpu.VMEM)
SMEM = pl.BlockSpec(memory_space=pltpu.SMEM)
ANY = pl.BlockSpec(memory_space=pl.ANY)
F32 = jnp.float32
BF16 = jnp.bfloat16


def partner(index, term):
    return index if term == 0 else index ^ (1 << (term - 1))


def send(value, term, routes):
    width = lax.axis_size("tensor")
    pairs = [
        (a * width + i, b * width + partner(i, term)) for a, b in routes for i in range(width)
    ]
    return lax.ppermute(value, AXES, pairs)


def column_chunks(width):
    return [(start, min(256, width - start)) for start in range(0, width, 256)]


def dot_nn(a, b):
    return lax.dot_general(a, b, (((1,), (0,)), ((), ())), preferred_element_type=F32)


def dot_nt(a, b):
    return lax.dot_general(a, b, (((1,), (1,)), ((), ())), preferred_element_type=F32)


def dot_tn(a, b):
    return lax.dot_general(a, b, (((0,), (0,)), ((), ())), preferred_element_type=F32)


def in_order(refs, order):
    by_term = dict(zip(order, refs))
    return [by_term[k] for k in range(len(refs))]


def forward_kernel(n, layer, last, order, rider, tokens, n_state, *refs):
    place, refs = refs[0], refs[1:]
    ins, refs = in_order(refs[:n], order), refs[n:]
    first, refs = refs[0], refs[1:]
    second, refs = refs[:n], refs[n:]
    riding, refs = (refs[0], refs[1:]) if rider is not None else (None, refs)
    refs = refs[n_state:]
    st_ins, st_pre, st_hid = refs[:3]
    outs, refs = (refs[3:3], refs[3:]) if last else (refs[3 : 3 + n], refs[3 + n :])
    preact, hidden, pieces, sems = refs
    rows = pl.ds(0, tokens)
    slab = ins[0].shape[1]

    @pl.when(place[0] == layer)
    def _():
        saves = [
            pltpu.make_async_copy(ins[k].at[rows], st_ins.at[k], sems.at[k]) for k in range(n)
        ]
        for copy in saves:
            copy.start()
        for start, size in column_chunks(preact.shape[1]):
            cols = slice(start, start + size)
            total = dot_nn(ins[0][rows, :], first[0, :, cols])
            for k in range(1, n):
                total = total + dot_nn(ins[k][rows, :], first[k, :, cols])
            preact[:, cols] = total
            inner = GELU_C * (total + GELU_A * (total * total * total))
            hidden[:, cols] = (0.5 * total * (1.0 + jnp.tanh(inner))).astype(BF16)
        save_pre = pltpu.make_async_copy(preact, st_pre, sems.at[n])
        save_pre.start()
        if not last:
            outs[0][...] = ins[0][rows, :].astype(F32) + dot_nt(hidden[...], second[0][...])
            for k in range(1, n):
                outs[k][...] = dot_nt(hidden[...], second[k][...]).astype(BF16)
        for c in range(pieces.shape[0]):
            pieces[c] = hidden[:, c * slab : (c + 1) * slab]
        save_hid = pltpu.make_async_copy(pieces, st_hid, sems.at[n + 1])
        save_hid.start()
        for copy in saves:
            copy.wait()
        save_pre.wait()
        save_hid.wait()

    if rider is not None:

        @pl.when(place[0] == rider)
        def _():
            for k in range(1, n):
                outs[k][...] = riding[...]


def idle_half(me, layer, half):
    return me < half if layer >= half else me >= half


def reduce_kernel(n, order, out_layer, n_state, *refs):
    place, terms, refs = refs[0], refs[1], refs[2:]
    got, refs = dict(zip(order, refs[: n - 1])), refs[n - 1 + n_state :]
    out, refs = refs[0], refs[1:]
    total = terms[...]
    for k in order:
        total = total + got[k][...].astype(F32)
    out[...] = total.astype(BF16)
    if out_layer is not None:
        st_out, sem = refs

        @pl.when(place[0] == out_layer)
        def _():
            copy = pltpu.make_async_copy(out, st_out, sem.at[0])
            copy.start()
            copy.wait()


def backward_kernel(n, layer, half, order, tokens, piece, earlier, n_state, *refs):
    place, refs = refs[0], refs[1:]
    ins, refs = in_order(refs[:n], order), refs[n:]
    first, refs = refs[0], refs[1:]
    second, refs = refs[:n], refs[n:]
    st_pre, st_hid, refs = refs[0], refs[1], refs[2:]
    got, refs = (refs[: n - 1], refs[n - 1 :]) if earlier is not None else (None, refs)
    refs = refs[n_state:]
    st_dpre, st_grad, st_near = refs[:3]
    outs, refs = refs[3 : 3 + n], refs[3 + n :]
    preact, dpre, sems = refs
    rows = pl.ds(0, tokens)

    @pl.when(place[0] == layer)
    def _():
        from_pre = pltpu.make_async_copy(st_pre, preact, sems.at[0])
        from_pre.start()
        save_grad = pltpu.make_async_copy(ins[0].at[rows], st_grad, sems.at[1])
        save_grad.start()
        for start, size in column_chunks(preact.shape[1]):
            cols = slice(start, start + size)
            total = dot_nn(ins[0][rows, :], second[0][:, cols])
            for k in range(1, n):
                total = total + dot_nn(ins[k][rows, :], second[k][:, cols])
            if start == 0:
                from_pre.wait()
            x = preact[:, cols]
            square = x * x
            bent = jnp.tanh(GELU_C * (x + GELU_A * (square * x)))
            slope = 0.5 * (1.0 + bent) + 0.5 * x * (1.0 - bent * bent) * (
                GELU_C * (1.0 + 3.0 * GELU_A * square)
            )
            dpre[:, cols] = (total * slope).astype(BF16)
        save_dpre = pltpu.make_async_copy(dpre, st_dpre, sems.at[2])
        save_dpre.start()
        outs[0][...] = ins[0][rows, :].astype(F32) + dot_nt(dpre[...], first[0])
        for k in range(1, n):
            outs[k][...] = dot_nt(dpre[...], first[k]).astype(BF16)
        save_grad.wait()
        save_dpre.wait()

    @pl.when(idle_half(place[0], layer, half))
    def _():
        copies = [
            pltpu.make_async_copy(st_hid.at[piece], outs[k], sems.at[k]) for k in range(1, n)
        ]
        for copy in copies:
            copy.start()
        for copy in copies:
            copy.wait()

    if earlier is not None:

        @pl.when(idle_half(place[0], layer + 1, half))
        def _():
            copies = [
                pltpu.make_async_copy(got[k], st_near.at[earlier, k], sems.at[n + k])
                for k in range(n - 1)
            ]
            for copy in copies:
                copy.start()
            for copy in copies:
                copy.wait()


def grad_kernel(n, half, *refs):
    place, ins, dpre, own, near, refs = refs[0], refs[1], refs[2], refs[3], refs[4], refs[5:]
    got, grad, refs = refs[: n - 1], refs[n - 1], refs[n:]
    out_first, out_second, v_first, v_second, block, sems = refs
    n_pieces, slab = own.shape[0], own.shape[2]
    copies = []
    for k in range(n):
        v_first[k] = dot_tn(ins[k], dpre[...]).astype(BF16)
        copies.append(pltpu.make_async_copy(v_first.at[k], out_first.at[k], sems.at[k]))
        copies[-1].start()
    for k in range(n):
        for c in range(n_pieces):
            cols = slice(c * slab, (c + 1) * slab)
            if k == 0:
                block[:, cols] = own[c]
            elif c < n_pieces - 1:
                block[:, cols] = near[c, k - 1]
            else:
                block[:, cols] = jnp.where(place[0] >= half, got[k - 1][...], near[c, k - 1])
        v_second[k] = dot_tn(grad[...], block[...]).astype(BF16)
        copies.append(pltpu.make_async_copy(v_second.at[k], out_second.at[k], sems.at[n + k]))
        copies[-1].start()
    for copy in copies:
        copy.wait()


def body(x_in, cotangent, w_in, w_out):
    sections = lax.axis_size("pipe")
    n = lax.axis_size("tensor").bit_length()
    me = lax.axis_index("pipe")
    batches, tok_rows, slab = x_in.shape
    tokens = batches * tok_rows
    first = w_in[0]
    owned = jnp.swapaxes(w_out[0], 1, 2)
    hid = first.shape[2]
    n_pieces = hid // slab
    shape = jax.ShapeDtypeStruct
    cost = pl.CostEstimate(
        flops=4 * tokens * n * slab * hid, bytes_accessed=4 * n * slab * hid, transcendentals=0
    )
    params = pltpu.CompilerParams(vmem_limit_bytes=12 * 1024 * 1024)
    work = [pltpu.VMEM((tokens, hid), F32), pltpu.VMEM((tokens, hid), BF16)]
    term_shapes = [shape((tokens, slab), F32)] + [shape((tokens, slab), BF16)] * (n - 1)

    everyone = [(s, s) for s in range(sections)]
    order = [k for k in (3, 5, 2, 4, 1) if k < n]

    def exchange(values, routes):
        got = {k: send(values[k], k, routes) for k in order}
        return [got[k] for k in range(1, n)]

    def neighbours(layer, step):
        return [
            (s, s + step)
            for s in range(layer % 2, sections, 2)
            if 0 <= s + step < sections
        ]

    def reduced(terms, got, out_layer=None, state=()):
        saves = out_layer is not None
        return pl.pallas_call(
            functools.partial(reduce_kernel, n, order, out_layer, len(state)),
            out_shape=[shape((tokens, slab), BF16)] * (1 + saves),
            in_specs=[SMEM] + [VMEM] * n + [ANY] * len(state),
            out_specs=[VMEM] + [ANY] * saves,
            scratch_shapes=[pltpu.SemaphoreType.DMA((1,))] * saves,
            input_output_aliases={1 + n: 1} if state else {},
            compiler_params=params,
        )(place, terms[0], *[got[k - 1] for k in order], *state)

    half = sections // 2
    place = me.astype(jnp.int32).reshape(1)
    x = x_in.reshape(tokens, slab)
    cot = cotangent.reshape(tokens, slab)
    ins = [x] + exchange([x] * n, everyone)
    second = [owned[0]] + exchange(owned, everyone)
    operands = [k for k in (0, 1, 4, 2, 3, 5) if k < n]

    state = []
    for layer in range(sections):
        last = layer == sections - 1
        rider = sections - 1 if layer == 0 else None
        riding = [cot] if layer == 0 else []
        state_shapes = [
            shape((n, tokens, slab), BF16),
            shape((tokens, hid), F32),
            shape((n_pieces, tokens, slab), BF16),
        ]
        outs = [] if last else term_shapes
        results = pl.pallas_call(
            functools.partial(forward_kernel, n, layer, last, operands, rider, tokens, len(state)),
            out_shape=state_shapes + outs,
            in_specs=[SMEM] + [VMEM] * (2 * n + 1 + len(riding)) + [ANY] * len(state),
            out_specs=[ANY] * 3 + [VMEM] * len(outs),
            scratch_shapes=work
            + [pltpu.VMEM((n_pieces, tokens, slab), BF16), pltpu.SemaphoreType.DMA((n + 2,))],
            input_output_aliases={2 + 2 * n + len(riding) + i: i for i in range(len(state))},
            cost_estimate=cost,
            compiler_params=params,
        )(place, *[ins[k] for k in operands], first, *second, *riding, *state)
        state, terms = list(results[:3]), results[3:]
        if last:
            break
        got = exchange(terms, everyone)
        if layer == 0:
            first_grads = [cot] + got
        (out,) = reduced(terms, got)
        route = neighbours(layer, 1)
        ins = exchange([out] * n, route)
        ins = [send(out, 0, route)] + ins

    st_ins, st_pre, st_hid = state
    state = []
    got = []
    grads_in = first_grads
    st_out = []
    for layer in reversed(range(sections)):
        piece = (sections - 1 - layer) % half
        earlier = (piece - 1) % half if got else None
        results = pl.pallas_call(
            functools.partial(
                backward_kernel,
                n,
                layer,
                half,
                operands,
                tokens,
                piece,
                earlier,
                len(state),
            ),
            out_shape=[
                shape((tokens, hid), BF16),
                shape((tokens, slab), BF16),
                shape((n_pieces, n - 1, tokens, slab), BF16),
            ]
            + term_shapes,
            in_specs=[SMEM]
            + [VMEM] * (2 * n + 1)
            + [ANY] * 2
            + [VMEM] * len(got)
            + [ANY] * len(state),
            out_specs=[ANY] * 3 + [VMEM] * n,
            scratch_shapes=work + [pltpu.SemaphoreType.DMA((2 * n,))],
            input_output_aliases={4 + 2 * n + len(got) + i: i for i in range(len(state))},
            cost_estimate=cost,
            compiler_params=params,
        )(
            place,
            *[grads_in[k] for k in operands],
            first,
            *second,
            st_pre,
            st_hid,
            *got,
            *state,
        )
        state, terms = list(results[:3]), results[3:]
        got = exchange(terms, everyone)
        out, st_out = reduced(terms, got, layer, st_out)
        st_out = [st_out]
        if layer > 0:
            route = neighbours(layer, -1)
            grads_in = exchange([out] * n, route)
            grads_in = [send(out, 0, route)] + grads_in

    st_dpre, st_grad, st_near = state
    grad_first, grad_second = pl.pallas_call(
        functools.partial(grad_kernel, n, half),
        out_shape=[shape((n, slab, hid), BF16)] * 2,
        in_specs=[SMEM] + [VMEM] * (4 + n),
        out_specs=[ANY] * 2,
        scratch_shapes=[pltpu.VMEM((n, slab, hid), BF16)] * 2
        + [pltpu.VMEM((tokens, hid), BF16), pltpu.SemaphoreType.DMA((2 * n,))],
        cost_estimate=cost,
        compiler_params=params,
    )(place, st_ins, st_dpre, st_hid, st_near, *got, st_grad)
    acts = st_out[0].reshape(batches, tok_rows, slab)
    return acts[None], grad_first[None], jnp.swapaxes(grad_second, 1, 2)[None]


def solution(mesh):
    placed = (
        P(None, None, "tensor"),
        P(None, None, "tensor"),
        P("pipe", None, None, "tensor"),
        P("pipe", None, None, "tensor"),
    )
    return jax.shard_map(
        body,
        mesh=mesh,
        in_specs=placed,
        out_specs=(P("pipe", None, None, "tensor"),) * 3,
        check_vma=False,
    )
```

```python
import functools

import jax
import jax.numpy as jnp
from jax import lax
from jax.experimental import pallas as pl
from jax.experimental.pallas import tpu as pltpu
from jax.sharding import PartitionSpec as P

AXES = ("pipe", "tensor")
GELU_C = 0.7978845608028654
GELU_A = 0.044715
VMEM = pl.BlockSpec(memory_space=pltpu.VMEM)
SMEM = pl.BlockSpec(memory_space=pltpu.SMEM)
ANY = pl.BlockSpec(memory_space=pl.ANY)
F32 = jnp.float32
BF16 = jnp.bfloat16


def partner(index, term):
    return index if term == 0 else index ^ (1 << (term - 1))


def send(value, term, routes):
    width = lax.axis_size("tensor")
    pairs = [
        (a * width + i, b * width + partner(i, term)) for a, b in routes for i in range(width)
    ]
    return lax.ppermute(value, AXES, pairs)


def turn_back(value, ring, distance):
    width = lax.axis_size("tensor")
    pairs = [
        (s * width + i, s * width + i // ring * ring + (i - distance) % ring)
        for s in range(lax.axis_size("pipe"))
        for i in range(width)
    ]
    return lax.ppermute(value, AXES, pairs)


def column_chunks(width):
    return [(start, min(256, width - start)) for start in range(0, width, 256)]


def dot_nn(a, b):
    return lax.dot_general(a, b, (((1,), (0,)), ((), ())), preferred_element_type=F32)


def dot_nt(a, b):
    return lax.dot_general(a, b, (((1,), (1,)), ((), ())), preferred_element_type=F32)


def dot_tn(a, b):
    return lax.dot_general(a, b, (((0,), (0,)), ((), ())), preferred_element_type=F32)


def split_kernel(far, *refs):
    owned, outs, sems = refs[0], refs[1:-1], refs[-1]
    half = owned.shape[1] // 2
    sources = [owned.at[far, pl.ds(0, half)], owned.at[far, pl.ds(half, half)]]
    sources += [owned.at[k] for k in range(owned.shape[0]) if k != far]
    copies = [
        pltpu.make_async_copy(source, out, sems.at[i])
        for i, (source, out) in enumerate(zip(sources, outs))
    ]
    for copy in copies:
        copy.start()
    for copy in copies:
        copy.wait()


def join_kernel(far, *refs):
    ins, out, sems = refs[:-2], refs[-2], refs[-1]
    half = ins[0].shape[0]
    places = [out.at[far, pl.ds(0, half)], out.at[far, pl.ds(half, half)]]
    places += [out.at[k] for k in range(out.shape[0]) if k != far]
    copies = [
        pltpu.make_async_copy(source, place, sems.at[i])
        for i, (source, place) in enumerate(zip(ins, places))
    ]
    for copy in copies:
        copy.start()
    for copy in copies:
        copy.wait()


def in_order(refs, order):
    by_term = dict(zip(order, refs))
    return [by_term[k] for k in range(len(refs))]


def forward_kernel(n, layer, last, order, rider, tokens, n_state, *refs):
    place, refs = refs[0], refs[1:]
    ins, refs = in_order(refs[:n], order), refs[n:]
    first, second, refs = refs[0], refs[1], refs[2:]
    riding, refs = (refs[0], refs[1:]) if rider is not None else (None, refs)
    refs = refs[n_state:]
    st_ins, st_pre, st_hid = refs[:3]
    outs, refs = (refs[3:3], refs[3:]) if last else (refs[3 : 3 + n], refs[3 + n :])
    preact, hidden, pieces, sems = refs
    rows = pl.ds(0, tokens)
    slab = ins[0].shape[1]

    @pl.when(place[0] == layer)
    def _():
        saves = [
            pltpu.make_async_copy(ins[k].at[rows], st_ins.at[k], sems.at[k]) for k in range(n)
        ]
        for copy in saves:
            copy.start()
        for start, size in column_chunks(preact.shape[1]):
            cols = slice(start, start + size)
            total = dot_nn(ins[0][rows, :], first[0, :, cols])
            for k in range(1, n):
                total = total + dot_nn(ins[k][rows, :], first[k, :, cols])
            preact[:, cols] = total
            inner = GELU_C * (total + GELU_A * (total * total * total))
            hidden[:, cols] = (0.5 * total * (1.0 + jnp.tanh(inner))).astype(BF16)
        save_pre = pltpu.make_async_copy(preact, st_pre, sems.at[n])
        save_pre.start()
        if not last:
            outs[0][...] = ins[0][rows, :].astype(F32) + dot_nt(hidden[...], second[0])
            for k in range(1, n):
                outs[k][...] = dot_nt(hidden[...], second[k]).astype(BF16)
        for c in range(pieces.shape[0]):
            pieces[c] = hidden[:, c * slab : (c + 1) * slab]
        save_hid = pltpu.make_async_copy(pieces, st_hid, sems.at[n + 1])
        save_hid.start()
        for copy in saves:
            copy.wait()
        save_pre.wait()
        save_hid.wait()

    if rider is not None:

        @pl.when(place[0] == rider)
        def _():
            for k in range(1, n):
                outs[k][...] = riding[...]


def idle_half(me, layer, half):
    return me < half if layer >= half else me >= half


def reduce_kernel(n, order, out_layer, n_state, *refs):
    place, terms, refs = refs[0], refs[1], refs[2:]
    got, refs = dict(zip(order, refs[: n - 1])), refs[n - 1 + n_state :]
    out, refs = refs[0], refs[1:]
    total = terms[...]
    for k in order:
        total = total + got[k][...].astype(F32)
    out[...] = total.astype(BF16)
    if out_layer is not None:
        st_out, sem = refs

        @pl.when(place[0] == out_layer)
        def _():
            copy = pltpu.make_async_copy(out, st_out, sem.at[0])
            copy.start()
            copy.wait()


def backward_kernel(n, layer, half, order, tokens, piece, earlier, n_state, *refs):
    place, refs = refs[0], refs[1:]
    ins, refs = in_order(refs[:n], order), refs[n:]
    first, second, refs = refs[0], refs[1], refs[2:]
    st_pre, st_hid, refs = refs[0], refs[1], refs[2:]
    got, refs = (refs[: n - 1], refs[n - 1 :]) if earlier is not None else (None, refs)
    refs = refs[n_state:]
    st_dpre, st_grad, st_near = refs[:3]
    outs, refs = refs[3 : 3 + n], refs[3 + n :]
    preact, dpre, sems = refs
    rows = pl.ds(0, tokens)

    @pl.when(place[0] == layer)
    def _():
        from_pre = pltpu.make_async_copy(st_pre, preact, sems.at[0])
        from_pre.start()
        save_grad = pltpu.make_async_copy(ins[0].at[rows], st_grad, sems.at[1])
        save_grad.start()
        for start, size in column_chunks(preact.shape[1]):
            cols = slice(start, start + size)
            total = dot_nn(ins[0][rows, :], second[0, :, cols])
            for k in range(1, n):
                total = total + dot_nn(ins[k][rows, :], second[k, :, cols])
            if start == 0:
                from_pre.wait()
            x = preact[:, cols]
            square = x * x
            bent = jnp.tanh(GELU_C * (x + GELU_A * (square * x)))
            slope = 0.5 * (1.0 + bent) + 0.5 * x * (1.0 - bent * bent) * (
                GELU_C * (1.0 + 3.0 * GELU_A * square)
            )
            dpre[:, cols] = (total * slope).astype(BF16)
        save_dpre = pltpu.make_async_copy(dpre, st_dpre, sems.at[2])
        save_dpre.start()
        outs[0][...] = ins[0][rows, :].astype(F32) + dot_nt(dpre[...], first[0])
        for k in range(1, n):
            outs[k][...] = dot_nt(dpre[...], first[k]).astype(BF16)
        save_grad.wait()
        save_dpre.wait()

    @pl.when(idle_half(place[0], layer, half))
    def _():
        copies = [
            pltpu.make_async_copy(st_hid.at[piece], outs[k], sems.at[k]) for k in range(1, n)
        ]
        for copy in copies:
            copy.start()
        for copy in copies:
            copy.wait()

    if earlier is not None:

        @pl.when(idle_half(place[0], layer + 1, half))
        def _():
            copies = [
                pltpu.make_async_copy(got[k], st_near.at[earlier, k], sems.at[n + k])
                for k in range(n - 1)
            ]
            for copy in copies:
                copy.start()
            for copy in copies:
                copy.wait()


def grad_kernel(n, half, *refs):
    place, ins, dpre, own, near, refs = refs[0], refs[1], refs[2], refs[3], refs[4], refs[5:]
    got, grad, refs = refs[: n - 1], refs[n - 1], refs[n:]
    out_first, out_second, v_first, v_second, block, sems = refs
    n_pieces, slab = own.shape[0], own.shape[2]
    copies = []
    for k in range(n):
        v_first[k] = dot_tn(ins[k], dpre[...]).astype(BF16)
        copies.append(pltpu.make_async_copy(v_first.at[k], out_first.at[k], sems.at[k]))
        copies[-1].start()
    for k in range(n):
        for c in range(n_pieces):
            cols = slice(c * slab, (c + 1) * slab)
            if k == 0:
                block[:, cols] = own[c]
            elif c < n_pieces - 1:
                block[:, cols] = near[c, k - 1]
            else:
                block[:, cols] = jnp.where(place[0] >= half, got[k - 1][...], near[c, k - 1])
        v_second[k] = dot_tn(grad[...], block[...]).astype(BF16)
        copies.append(pltpu.make_async_copy(v_second.at[k], out_second.at[k], sems.at[n + k]))
        copies[-1].start()
    for copy in copies:
        copy.wait()


def body(x_in, cotangent, w_in, w_out):
    sections = lax.axis_size("pipe")
    n = lax.axis_size("tensor").bit_length()
    me = lax.axis_index("pipe")
    batches, tok_rows, slab = x_in.shape
    tokens = batches * tok_rows
    first = w_in[0]
    owned = jnp.swapaxes(w_out[0], 1, 2)
    hid = first.shape[2]
    n_pieces = hid // slab
    shape = jax.ShapeDtypeStruct
    cost = pl.CostEstimate(
        flops=4 * tokens * n * slab * hid, bytes_accessed=4 * n * slab * hid, transcendentals=0
    )
    params = pltpu.CompilerParams(vmem_limit_bytes=12 * 1024 * 1024)
    work = [pltpu.VMEM((tokens, hid), F32), pltpu.VMEM((tokens, hid), BF16)]
    term_shapes = [shape((tokens, slab), F32)] + [shape((tokens, slab), BF16)] * (n - 1)

    everyone = [(s, s) for s in range(sections)]
    order = [k for k in (3, 5, 2, 4, 1) if k < n]

    def exchange(values, routes):
        got = {k: send(values[k], k, routes) for k in order}
        return [got[k] for k in range(1, n)]

    def neighbours(layer, step):
        return [
            (s, s + step)
            for s in range(layer % 2, sections, 2)
            if 0 <= s + step < sections
        ]

    def reduced(terms, got, out_layer=None, state=()):
        saves = out_layer is not None
        return pl.pallas_call(
            functools.partial(reduce_kernel, n, order, out_layer, len(state)),
            out_shape=[shape((tokens, slab), BF16)] * (1 + saves),
            in_specs=[SMEM] + [VMEM] * n + [ANY] * len(state),
            out_specs=[VMEM] + [ANY] * saves,
            scratch_shapes=[pltpu.SemaphoreType.DMA((1,))] * saves,
            input_output_aliases={1 + n: 1} if state else {},
            compiler_params=params,
        )(place, terms[0], *[got[k - 1] for k in order], *state)

    half = sections // 2
    place = me.astype(jnp.int32).reshape(1)
    x = x_in.reshape(tokens, slab)
    cot = cotangent.reshape(tokens, slab)
    ins = [x] + exchange([x] * n, everyone)
    far = 3
    low, high, *rest = pl.pallas_call(
        functools.partial(split_kernel, far),
        out_shape=[shape((slab // 2, hid), BF16)] * 2 + [shape((slab, hid), BF16)] * (n - 1),
        in_specs=[ANY],
        out_specs=[ANY] * (n + 1),
        scratch_shapes=[pltpu.SemaphoreType.DMA((n + 1,))],
        compiler_params=params,
    )(owned)
    blocks = dict(zip([k for k in range(n) if k != far], rest))
    high = turn_back(high, 8, 2)
    low = send(low, far, everyone)
    swapped = {k: send(blocks[k], k, everyone) for k in order if k != far}
    high = turn_back(high, 8, 2)
    pieces = [low, high, blocks[0]] + [swapped[k] for k in range(1, n) if k != far]
    (second,) = pl.pallas_call(
        functools.partial(join_kernel, far),
        out_shape=[shape((n, slab, hid), BF16)],
        in_specs=[ANY] * len(pieces),
        out_specs=[VMEM],
        scratch_shapes=[pltpu.SemaphoreType.DMA((n + 1,))],
        compiler_params=params,
    )(*pieces)
    operands = [k for k in (0, 1, 4, 2, 3, 5) if k < n]

    state = []
    for layer in range(sections):
        last = layer == sections - 1
        rider = sections - 1 if layer == 0 else None
        riding = [cot] if layer == 0 else []
        state_shapes = [
            shape((n, tokens, slab), BF16),
            shape((tokens, hid), F32),
            shape((n_pieces, tokens, slab), BF16),
        ]
        outs = [] if last else term_shapes
        results = pl.pallas_call(
            functools.partial(forward_kernel, n, layer, last, operands, rider, tokens, len(state)),
            out_shape=state_shapes + outs,
            in_specs=[SMEM] + [VMEM] * (n + 2 + len(riding)) + [ANY] * len(state),
            out_specs=[ANY] * 3 + [VMEM] * len(outs),
            scratch_shapes=work
            + [pltpu.VMEM((n_pieces, tokens, slab), BF16), pltpu.SemaphoreType.DMA((n + 2,))],
            input_output_aliases={3 + n + len(riding) + i: i for i in range(len(state))},
            cost_estimate=cost,
            compiler_params=params,
        )(place, *[ins[k] for k in operands], first, second, *riding, *state)
        state, terms = list(results[:3]), results[3:]
        if last:
            break
        got = exchange(terms, everyone)
        if layer == 0:
            first_grads = [cot] + got
        (out,) = reduced(terms, got)
        route = neighbours(layer, 1)
        ins = exchange([out] * n, route)
        ins = [send(out, 0, route)] + ins

    st_ins, st_pre, st_hid = state
    state = []
    got = []
    grads_in = first_grads
    st_out = []
    for layer in reversed(range(sections)):
        piece = (sections - 1 - layer) % half
        earlier = (piece - 1) % half if got else None
        results = pl.pallas_call(
            functools.partial(
                backward_kernel,
                n,
                layer,
                half,
                operands,
                tokens,
                piece,
                earlier,
                len(state),
            ),
            out_shape=[
                shape((tokens, hid), BF16),
                shape((tokens, slab), BF16),
                shape((n_pieces, n - 1, tokens, slab), BF16),
            ]
            + term_shapes,
            in_specs=[SMEM]
            + [VMEM] * (n + 2)
            + [ANY] * 2
            + [VMEM] * len(got)
            + [ANY] * len(state),
            out_specs=[ANY] * 3 + [VMEM] * n,
            scratch_shapes=work + [pltpu.SemaphoreType.DMA((2 * n,))],
            input_output_aliases={5 + n + len(got) + i: i for i in range(len(state))},
            cost_estimate=cost,
            compiler_params=params,
        )(
            place,
            *[grads_in[k] for k in operands],
            first,
            second,
            st_pre,
            st_hid,
            *got,
            *state,
        )
        state, terms = list(results[:3]), results[3:]
        got = exchange(terms, everyone)
        out, st_out = reduced(terms, got, layer, st_out)
        st_out = [st_out]
        if layer > 0:
            route = neighbours(layer, -1)
            grads_in = exchange([out] * n, route)
            grads_in = [send(out, 0, route)] + grads_in

    st_dpre, st_grad, st_near = state
    grad_first, grad_second = pl.pallas_call(
        functools.partial(grad_kernel, n, half),
        out_shape=[shape((n, slab, hid), BF16)] * 2,
        in_specs=[SMEM] + [VMEM] * (4 + n),
        out_specs=[ANY] * 2,
        scratch_shapes=[pltpu.VMEM((n, slab, hid), BF16)] * 2
        + [pltpu.VMEM((tokens, hid), BF16), pltpu.SemaphoreType.DMA((2 * n,))],
        cost_estimate=cost,
        compiler_params=params,
    )(place, st_ins, st_dpre, st_hid, st_near, *got, st_grad)
    acts = st_out[0].reshape(batches, tok_rows, slab)
    return acts[None], grad_first[None], jnp.swapaxes(grad_second, 1, 2)[None]


def solution(mesh):
    placed = (
        P(None, None, "tensor"),
        P(None, None, "tensor"),
        P("pipe", None, None, "tensor"),
        P("pipe", None, None, "tensor"),
    )
    return jax.shard_map(
        body,
        mesh=mesh,
        in_specs=placed,
        out_specs=(P("pipe", None, None, "tensor"),) * 3,
        check_vma=False,
    )
```

```python
import functools

import jax
import jax.numpy as jnp
from jax import lax
from jax.experimental import pallas as pl
from jax.experimental.pallas import tpu as pltpu
from jax.sharding import PartitionSpec as P

AXES = ("pipe", "tensor")
GELU_C = 0.7978845608028654
GELU_A = 0.044715
VMEM = pl.BlockSpec(memory_space=pltpu.VMEM)
SMEM = pl.BlockSpec(memory_space=pltpu.SMEM)
ANY = pl.BlockSpec(memory_space=pl.ANY)
F32 = jnp.float32
BF16 = jnp.bfloat16


def partner(index, term):
    return index if term == 0 else index ^ (1 << (term - 1))


def send(value, term, routes):
    width = lax.axis_size("tensor")
    pairs = [
        (a * width + i, b * width + partner(i, term)) for a, b in routes for i in range(width)
    ]
    return lax.ppermute(value, AXES, pairs)


def turn_back(value, ring, distance):
    width = lax.axis_size("tensor")
    pairs = [
        (s * width + i, s * width + i // ring * ring + (i - distance) % ring)
        for s in range(lax.axis_size("pipe"))
        for i in range(width)
    ]
    return lax.ppermute(value, AXES, pairs)


def column_chunks(width):
    return [(start, min(256, width - start)) for start in range(0, width, 256)]


def dot_nn(a, b):
    return lax.dot_general(a, b, (((1,), (0,)), ((), ())), preferred_element_type=F32)


def dot_nt(a, b):
    return lax.dot_general(a, b, (((1,), (1,)), ((), ())), preferred_element_type=F32)


def dot_tn(a, b):
    return lax.dot_general(a, b, (((0,), (0,)), ((), ())), preferred_element_type=F32)


def split_kernel(far, *refs):
    owned, outs, sems = refs[0], refs[1:-1], refs[-1]
    half = owned.shape[1] // 2
    sources = [owned.at[far, pl.ds(0, half)], owned.at[far, pl.ds(half, half)]]
    sources += [owned.at[k] for k in range(owned.shape[0]) if k != far]
    copies = [
        pltpu.make_async_copy(source, out, sems.at[i])
        for i, (source, out) in enumerate(zip(sources, outs))
    ]
    for copy in copies:
        copy.start()
    for copy in copies:
        copy.wait()


def join_kernel(far, *refs):
    ins, out, sems = refs[:-2], refs[-2], refs[-1]
    half = ins[0].shape[0]
    places = [out.at[far, pl.ds(0, half)], out.at[far, pl.ds(half, half)]]
    places += [out.at[k] for k in range(out.shape[0]) if k != far]
    copies = [
        pltpu.make_async_copy(source, place, sems.at[i])
        for i, (source, place) in enumerate(zip(ins, places))
    ]
    for copy in copies:
        copy.start()
    for copy in copies:
        copy.wait()


def in_order(refs, order):
    by_term = dict(zip(order, refs))
    return [by_term[k] for k in range(len(refs))]


def forward_kernel(n, layer, last, order, rider, tokens, n_state, *refs):
    place, refs = refs[0], refs[1:]
    ins, refs = in_order(refs[:n], order), refs[n:]
    first, second, refs = refs[0], refs[1], refs[2:]
    riding, refs = (refs[0], refs[1:]) if rider is not None else (None, refs)
    refs = refs[n_state:]
    st_ins, st_pre, st_hid = refs[:3]
    outs, refs = (refs[3:3], refs[3:]) if last else (refs[3 : 3 + n], refs[3 + n :])
    preact, hidden, pieces, sems = refs
    rows = pl.ds(0, tokens)
    slab = ins[0].shape[1]

    @pl.when(place[0] == layer)
    def _():
        saves = [
            pltpu.make_async_copy(ins[k].at[rows], st_ins.at[k], sems.at[k]) for k in range(n)
        ]
        for copy in saves:
            copy.start()
        for start, size in column_chunks(preact.shape[1]):
            cols = slice(start, start + size)
            total = dot_nn(ins[0][rows, :], first[0, :, cols])
            for k in range(1, n):
                total = total + dot_nn(ins[k][rows, :], first[k, :, cols])
            preact[:, cols] = total
            inner = GELU_C * (total + GELU_A * (total * total * total))
            hidden[:, cols] = (0.5 * total * (1.0 + jnp.tanh(inner))).astype(BF16)
        save_pre = pltpu.make_async_copy(preact, st_pre, sems.at[n])
        save_pre.start()
        if not last:
            outs[0][...] = ins[0][rows, :].astype(F32) + dot_nt(hidden[...], second[0])
            for k in range(1, n):
                outs[k][...] = dot_nt(hidden[...], second[k]).astype(BF16)
        for c in range(pieces.shape[0]):
            pieces[c] = hidden[:, c * slab : (c + 1) * slab]
        save_hid = pltpu.make_async_copy(pieces, st_hid, sems.at[n + 1])
        save_hid.start()
        for copy in saves:
            copy.wait()
        save_pre.wait()
        save_hid.wait()

    if rider is not None:

        @pl.when(place[0] == rider)
        def _():
            for k in range(1, n):
                outs[k][...] = riding[...]


def idle_half(me, layer, half):
    return me < half if layer >= half else me >= half


def reduce_kernel(n, order, out_layer, n_state, *refs):
    place, terms, refs = refs[0], refs[1], refs[2:]
    got, refs = dict(zip(order, refs[: n - 1])), refs[n - 1 + n_state :]
    out, refs = refs[0], refs[1:]
    total = terms[...]
    for k in order:
        total = total + got[k][...].astype(F32)
    out[...] = total.astype(BF16)
    if out_layer is not None:
        st_out, sem = refs

        @pl.when(place[0] == out_layer)
        def _():
            copy = pltpu.make_async_copy(out, st_out, sem.at[0])
            copy.start()
            copy.wait()


def backward_kernel(n, layer, half, order, tokens, piece, earlier, n_state, *refs):
    place, refs = refs[0], refs[1:]
    ins, refs = in_order(refs[:n], order), refs[n:]
    first, second, refs = refs[0], refs[1], refs[2:]
    st_pre, st_hid, refs = refs[0], refs[1], refs[2:]
    got, refs = (refs[: n - 1], refs[n - 1 :]) if earlier is not None else (None, refs)
    refs = refs[n_state:]
    st_dpre, st_grad, st_near = refs[:3]
    outs, refs = refs[3 : 3 + n], refs[3 + n :]
    preact, dpre, sems = refs
    rows = pl.ds(0, tokens)

    @pl.when(place[0] == layer)
    def _():
        from_pre = pltpu.make_async_copy(st_pre, preact, sems.at[0])
        from_pre.start()
        save_grad = pltpu.make_async_copy(ins[0].at[rows], st_grad, sems.at[1])
        save_grad.start()
        for start, size in column_chunks(preact.shape[1]):
            cols = slice(start, start + size)
            total = dot_nn(ins[0][rows, :], second[0, :, cols])
            for k in range(1, n):
                total = total + dot_nn(ins[k][rows, :], second[k, :, cols])
            if start == 0:
                from_pre.wait()
            x = preact[:, cols]
            square = x * x
            bent = jnp.tanh(GELU_C * (x + GELU_A * (square * x)))
            slope = 0.5 * (1.0 + bent) + 0.5 * x * (1.0 - bent * bent) * (
                GELU_C * (1.0 + 3.0 * GELU_A * square)
            )
            dpre[:, cols] = (total * slope).astype(BF16)
        save_dpre = pltpu.make_async_copy(dpre, st_dpre, sems.at[2])
        save_dpre.start()
        outs[0][...] = ins[0][rows, :].astype(F32) + dot_nt(dpre[...], first[0])
        for k in range(1, n):
            outs[k][...] = dot_nt(dpre[...], first[k]).astype(BF16)
        save_grad.wait()
        save_dpre.wait()

    @pl.when(idle_half(place[0], layer, half))
    def _():
        copies = [
            pltpu.make_async_copy(st_hid.at[piece], outs[k], sems.at[k]) for k in range(1, n)
        ]
        for copy in copies:
            copy.start()
        for copy in copies:
            copy.wait()

    if earlier is not None:

        @pl.when(idle_half(place[0], layer + 1, half))
        def _():
            copies = [
                pltpu.make_async_copy(got[k], st_near.at[earlier, k], sems.at[n + k])
                for k in range(n - 1)
            ]
            for copy in copies:
                copy.start()
            for copy in copies:
                copy.wait()


def grad_kernel(n, half, *refs):
    place, ins, dpre, own, near, refs = refs[0], refs[1], refs[2], refs[3], refs[4], refs[5:]
    got, grad, refs = refs[: n - 1], refs[n - 1], refs[n:]
    out_first, out_second, v_first, v_second, block, sems = refs
    n_pieces, slab = own.shape[0], own.shape[2]
    copies = []
    for k in range(n):
        v_first[k] = dot_tn(ins[k], dpre[...]).astype(BF16)
        copies.append(pltpu.make_async_copy(v_first.at[k], out_first.at[k], sems.at[k]))
        copies[-1].start()
    for k in range(n):
        for c in range(n_pieces):
            cols = slice(c * slab, (c + 1) * slab)
            if k == 0:
                block[:, cols] = own[c]
            elif c < n_pieces - 1:
                block[:, cols] = near[c, k - 1]
            else:
                block[:, cols] = jnp.where(place[0] >= half, got[k - 1][...], near[c, k - 1])
        v_second[k] = dot_tn(grad[...], block[...]).astype(BF16)
        copies.append(pltpu.make_async_copy(v_second.at[k], out_second.at[k], sems.at[n + k]))
        copies[-1].start()
    for copy in copies:
        copy.wait()


def body(x_in, cotangent, w_in, w_out):
    sections = lax.axis_size("pipe")
    n = lax.axis_size("tensor").bit_length()
    me = lax.axis_index("pipe")
    batches, tok_rows, slab = x_in.shape
    tokens = batches * tok_rows
    first = w_in[0]
    owned = jnp.swapaxes(w_out[0], 1, 2)
    hid = first.shape[2]
    n_pieces = hid // slab
    shape = jax.ShapeDtypeStruct
    cost = pl.CostEstimate(
        flops=4 * tokens * n * slab * hid, bytes_accessed=4 * n * slab * hid, transcendentals=0
    )
    params = pltpu.CompilerParams(vmem_limit_bytes=12 * 1024 * 1024)
    work = [pltpu.VMEM((tokens, hid), F32), pltpu.VMEM((tokens, hid), BF16)]
    term_shapes = [shape((tokens, slab), F32)] + [shape((tokens, slab), BF16)] * (n - 1)

    everyone = [(s, s) for s in range(sections)]
    order = [k for k in (2, 3, 5, 4, 1) if k < n]

    def exchange(values, routes):
        got = {k: send(values[k], k, routes) for k in order}
        return [got[k] for k in range(1, n)]

    def neighbours(layer, step):
        return [
            (s, s + step)
            for s in range(layer % 2, sections, 2)
            if 0 <= s + step < sections
        ]

    def reduced(terms, got, out_layer=None, state=()):
        saves = out_layer is not None
        return pl.pallas_call(
            functools.partial(reduce_kernel, n, order, out_layer, len(state)),
            out_shape=[shape((tokens, slab), BF16)] * (1 + saves),
            in_specs=[SMEM] + [VMEM] * n + [ANY] * len(state),
            out_specs=[VMEM] + [ANY] * saves,
            scratch_shapes=[pltpu.SemaphoreType.DMA((1,))] * saves,
            input_output_aliases={1 + n: 1} if state else {},
            compiler_params=params,
        )(place, terms[0], *[got[k - 1] for k in order], *state)

    half = sections // 2
    place = me.astype(jnp.int32).reshape(1)
    x = x_in.reshape(tokens, slab)
    cot = cotangent.reshape(tokens, slab)
    ins = [x] + exchange([x] * n, everyone)
    owned, *ins = lax.optimization_barrier((owned, *ins))
    far = 3
    low, high, *rest = pl.pallas_call(
        functools.partial(split_kernel, far),
        out_shape=[shape((slab // 2, hid), BF16)] * 2 + [shape((slab, hid), BF16)] * (n - 1),
        in_specs=[ANY],
        out_specs=[ANY] * (n + 1),
        scratch_shapes=[pltpu.SemaphoreType.DMA((n + 1,))],
        compiler_params=params,
    )(owned)
    blocks = dict(zip([k for k in range(n) if k != far], rest))
    high = turn_back(high, 8, 2)
    low = send(low, far, everyone)
    swapped = {k: send(blocks[k], k, everyone) for k in order if k != far}
    high = turn_back(high, 8, 2)
    pieces = [low, high, blocks[0]] + [swapped[k] for k in range(1, n) if k != far]
    (second,) = pl.pallas_call(
        functools.partial(join_kernel, far),
        out_shape=[shape((n, slab, hid), BF16)],
        in_specs=[ANY] * len(pieces),
        out_specs=[VMEM],
        scratch_shapes=[pltpu.SemaphoreType.DMA((n + 1,))],
        compiler_params=params,
    )(*pieces)
    operands = [k for k in (0, 1, 4, 5, 3, 2) if k < n]

    state = []
    for layer in range(sections):
        last = layer == sections - 1
        rider = sections - 1 if layer == 0 else None
        riding = [cot] if layer == 0 else []
        state_shapes = [
            shape((n, tokens, slab), BF16),
            shape((tokens, hid), F32),
            shape((n_pieces, tokens, slab), BF16),
        ]
        outs = [] if last else term_shapes
        results = pl.pallas_call(
            functools.partial(forward_kernel, n, layer, last, operands, rider, tokens, len(state)),
            out_shape=state_shapes + outs,
            in_specs=[SMEM] + [VMEM] * (n + 2 + len(riding)) + [ANY] * len(state),
            out_specs=[ANY] * 3 + [VMEM] * len(outs),
            scratch_shapes=work
            + [pltpu.VMEM((n_pieces, tokens, slab), BF16), pltpu.SemaphoreType.DMA((n + 2,))],
            input_output_aliases={3 + n + len(riding) + i: i for i in range(len(state))},
            cost_estimate=cost,
            compiler_params=params,
        )(place, *[ins[k] for k in operands], first, second, *riding, *state)
        state, terms = list(results[:3]), results[3:]
        if last:
            break
        got = exchange(terms, everyone)
        if layer == 0:
            first_grads = [cot] + got
        (out,) = reduced(terms, got)
        route = neighbours(layer, 1)
        ins = exchange([out] * n, route)
        ins = [send(out, 0, route)] + ins

    st_ins, st_pre, st_hid = state
    state = []
    got = []
    grads_in = first_grads
    st_out = []
    for layer in reversed(range(sections)):
        piece = (sections - 1 - layer) % half
        earlier = (piece - 1) % half if got else None
        results = pl.pallas_call(
            functools.partial(
                backward_kernel,
                n,
                layer,
                half,
                operands,
                tokens,
                piece,
                earlier,
                len(state),
            ),
            out_shape=[
                shape((tokens, hid), BF16),
                shape((tokens, slab), BF16),
                shape((n_pieces, n - 1, tokens, slab), BF16),
            ]
            + term_shapes,
            in_specs=[SMEM]
            + [VMEM] * (n + 2)
            + [ANY] * 2
            + [VMEM] * len(got)
            + [ANY] * len(state),
            out_specs=[ANY] * 3 + [VMEM] * n,
            scratch_shapes=work + [pltpu.SemaphoreType.DMA((2 * n,))],
            input_output_aliases={5 + n + len(got) + i: i for i in range(len(state))},
            cost_estimate=cost,
            compiler_params=params,
        )(
            place,
            *[grads_in[k] for k in operands],
            first,
            second,
            st_pre,
            st_hid,
            *got,
            *state,
        )
        state, terms = list(results[:3]), results[3:]
        got = exchange(terms, everyone)
        out, st_out = reduced(terms, got, layer, st_out)
        st_out = [st_out]
        if layer > 0:
            route = neighbours(layer, -1)
            grads_in = exchange([out] * n, route)
            grads_in = [send(out, 0, route)] + grads_in

    st_dpre, st_grad, st_near = state
    grad_first, grad_second = pl.pallas_call(
        functools.partial(grad_kernel, n, half),
        out_shape=[shape((n, slab, hid), BF16)] * 2,
        in_specs=[SMEM] + [VMEM] * (4 + n),
        out_specs=[ANY] * 2,
        scratch_shapes=[pltpu.VMEM((n, slab, hid), BF16)] * 2
        + [pltpu.VMEM((tokens, hid), BF16), pltpu.SemaphoreType.DMA((2 * n,))],
        cost_estimate=cost,
        compiler_params=params,
    )(place, st_ins, st_dpre, st_hid, st_near, *got, st_grad)
    acts = st_out[0].reshape(batches, tok_rows, slab)
    return acts[None], grad_first[None], jnp.swapaxes(grad_second, 1, 2)[None]


def solution(mesh):
    placed = (
        P(None, None, "tensor"),
        P(None, None, "tensor"),
        P("pipe", None, None, "tensor"),
        P("pipe", None, None, "tensor"),
    )
    return jax.shard_map(
        body,
        mesh=mesh,
        in_specs=placed,
        out_specs=(P("pipe", None, None, "tensor"),) * 3,
        check_vma=False,
    )
```
